32 devices in a mesh: group: 2 (over y), comp: 4 (over z), sub: 4 (over x, core).
Axes of the slice: x: 2, y: 2, z: 4, core: 2. Of those that a mesh axis runs over, the one named last changes fastest.
Arguments:
- wind_u: bfloat16 [72, 131072], P(None, ('group', 'comp', 'sub')), parts along dimension 1, may hold values from 2 to 3
- wind_v: bfloat16 [72, 131072], P(None, ('group', 'comp', 'sub')), parts along dimension 1, may hold values from -3 to 3
- buoyancy_freq: bfloat16 [72, 131072], P(None, ('group', 'comp', 'sub')), parts along dimension 1, may hold values from 0.796875 to 1.25
- air_density: bfloat16 [72, 131072], P(None, ('group', 'comp', 'sub')), parts along dimension 1, may hold values from 0.0125 to 1.3
- layer_mass: bfloat16 [72, 131072], P(None, ('group', 'comp', 'sub')), parts along dimension 1, may hold values from 0.5 to 2
- orography: float32 [65536], P(('comp', 'sub')), may hold values from 0.2 to 1.5
- surface_flux: float32 [6, 131072], P(None, ('group', 'comp', 'sub')), parts along dimension 1, may hold values from -6 to 6
- send_list: int32 [16, 16, 2048], P(('comp', 'sub')), may hold values from 0 to 4095, as said below
- depth: float32 [512, 1024], P('comp', 'sub'), may hold values from 0.5 to 1.5
- ocean_state: float32 [5, 1024, 1024], P(None, ('group', 'comp'), 'sub'), parts along dimension 1, may hold values from -3 to 3
- map_slot: int32 [4, 512, 1024], P(None, 'comp', 'sub'), may hold values from 0 to 32767, as said below
- map_weight: float32 [4, 512, 1024], P(None, 'comp', 'sub'), may hold values from 0.1 to 0.5
Outputs:
- drag_tendency: bfloat16 [2, 72, 131072], P(None, None, ('group', 'comp', 'sub')), parts along dimension 2
- ocean_out: float32 [5, 1024, 1024], P(None, ('group', 'comp'), 'sub'), parts along dimension 1
The draws below stay inside these ranges and needn't reach their ends.
There are 2 independent parts, one for each index of `group`. The reference program is written for one: setup_inputs(seed, part) draws one part's arguments, and reference() takes and returns one part's arrays. A program takes and returns all parts, laid end to end along the dimension named above; an argument that names none is the same for every part. Nothing has to cross between parts.
Inputs may be any that keep to these rules, and one draw needn't show every extreme that they name: Each entry names a column within the source device's block of 4096 columns; with q = d * 2048 + c, the entry send_list[s, d, c] lies in the block of 128 columns numbered (q // 128) % 32. `map_slot`: each entry names a slot that the cell's device receives, numbered source device times 2048 plus slot; for the cell at local row r and local column t of its device, with p = r * 256 + t, the slot lies in 128 * (p // 128) to 128 * (p // 128) + 127.
All inputs are finite; a program needn't handle non-finite values.
Results may differ from the reference program's by a relative error of at most 0.001.
Values sent between devices are 32-bit elements; how exact they have to be, the bound alone decides.
A program may use at most 64 MiB of HBM per device.

```python
import math
import jax
import jax.numpy as jnp
from jax import lax

L = 72
A_DEV = 4096
OY = 128
OX = 256
K = 4
SUBCYCLES = 8
CAP = 2048
ACOLS = 65536
NOY = 512
NOX = 1024
N_COMP = 4
N_SUB = 4


def draw_air_density(key, part):
    key = jax.random.fold_in(key, 11)
    level_idx = jnp.arange(L, dtype=jnp.float32)[:, None]
    jitter = jax.random.uniform(key, (L, ACOLS), jnp.float32, 0.7, 1.3)
    return (jnp.exp(-4.0 * level_idx / L) * jitter).astype(jnp.bfloat16)


def draw_send_list(key, part):
    key = jax.random.fold_in(key, 23)
    devices = N_COMP * N_SUB
    blocks_src = A_DEV // 128
    flat_slot = jnp.arange(devices, dtype=jnp.int32)[:, None] * CAP + jnp.arange(CAP, dtype=jnp.int32)[None, :]
    col_block = flat_slot // 128 % blocks_src
    inside = jax.random.randint(key, (devices, devices, CAP), 0, 128, dtype=jnp.int32)
    top_slot = (flat_slot == blocks_src * 128 - 1)[None]
    low_slot = (flat_slot == 0)[None]
    inside = jnp.where(top_slot, 127, jnp.where(low_slot, 0, inside))
    return (col_block[None] * 128 + inside).astype(jnp.int32)


def draw_map_slot(key, part):
    key = jax.random.fold_in(key, 37)
    row_local = jnp.arange(NOY, dtype=jnp.int32) % OY
    col_local = jnp.arange(NOX, dtype=jnp.int32) % OX
    flat_cell = row_local[:, None] * OX + col_local[None, :]
    inside = jax.random.randint(key, (K, NOY, NOX), 0, 128, dtype=jnp.int32)
    entry_first = (jnp.arange(K, dtype=jnp.int32) == 0)[:, None, None]
    top_cell = entry_first & (flat_cell == OY * OX - 1)[None]
    low_cell = entry_first & (flat_cell == 0)[None]
    inside = jnp.where(top_cell, 127, jnp.where(low_cell, 0, inside))
    return (flat_cell // 128 * 128 + inside).astype(jnp.int32)


def block_scale(rng, extent, split, low, high):
    loudness = 1.0
    for position, blocks in split:
        heights = jax.random.uniform(jax.random.fold_in(jax.random.fold_in(rng, 6), position), (blocks,), jnp.float32, low / len(split), high / len(split))
        loudness = loudness * jnp.repeat(jnp.exp(heights), extent[position] // blocks).reshape((-1,) + (1,) * (len(extent) - 1 - position))
    return loudness


def gaussian(own_key, shape, width, most, pieces=(), held_as=jnp.bfloat16):
    gain = block_scale(own_key, shape, pieces, -0.22, 0.18) if pieces else 1.0
    values = jax.random.normal(own_key, shape, jnp.float32) * width * gain
    return jnp.minimum(jnp.maximum(values, -most), most).astype(held_as)


def setup_inputs(seed: int = 0, part: int = 0) -> dict:
    key_list = jax.random.split(jax.random.key(seed), 13)
    part_keys = jax.random.split(jax.random.fold_in(key_list[12], part), 13)
    wind_u = jnp.clip(2.0 + 1.0 * jax.random.uniform(part_keys[0], (L, ACOLS), jnp.float32) ** block_scale(part_keys[0], (L, ACOLS), ((1, 16),), -0.2, 0.2), 2.0, 3.0).astype(jnp.bfloat16)
    wind_v = gaussian(part_keys[1], (L, ACOLS), 0.5, 3.0, ((1, 16),))
    buoyancy_freq = jnp.clip(jnp.exp(math.log(1.25) - 0.450201 * jax.random.uniform(part_keys[2], (L, ACOLS), jnp.float32) ** block_scale(part_keys[2], (L, ACOLS), ((1, 16),), -0.2, 0.2)), 0.796875, 1.25).astype(jnp.bfloat16)
    air_density = draw_air_density(jax.random.fold_in(jax.random.fold_in(key_list[12], part), 71), part)
    layer_mass = jnp.clip(jnp.exp(math.log(2.0) - 1.3862944 * jax.random.uniform(part_keys[4], (L, ACOLS), jnp.float32) ** block_scale(part_keys[4], (L, ACOLS), ((1, 16),), -0.2, 0.2)), 0.5, 2.0).astype(jnp.bfloat16)
    orography = jnp.clip(jnp.exp(math.log(1.5) - 2.014903 * jax.random.uniform(key_list[5], (ACOLS,), jnp.float32) ** block_scale(key_list[5], (ACOLS,), ((0, 16),), -0.2, 0.2)), 0.2, 1.5)
    surface_flux = gaussian(part_keys[6], (6, ACOLS), 1.0, 6.0, ((1, 16),), jnp.float32)
    send_list = draw_send_list(jax.random.fold_in(key_list[12], 71), part)
    depth = jnp.clip(0.5 + 1.0 * jax.random.uniform(key_list[8], (NOY, NOX), jnp.float32) ** block_scale(key_list[8], (NOY, NOX), ((0, 4), (1, 4)), -0.2, 0.2), 0.5, 1.5)
    ocean_state = gaussian(part_keys[9], (5, NOY, NOX), 0.5, 3.0, ((1, 4), (2, 4)), jnp.float32)
    map_slot = draw_map_slot(jax.random.fold_in(key_list[12], 71), part)
    map_weight = jnp.clip(0.1 + 0.4 * jax.random.uniform(key_list[11], (K, NOY, NOX), jnp.float32) ** block_scale(key_list[11], (K, NOY, NOX), ((1, 4), (2, 4)), -0.2, 0.2), 0.1, 0.5)
    return {"wind_u": wind_u, "wind_v": wind_v, "buoyancy_freq": buoyancy_freq, "air_density": air_density, "layer_mass": layer_mass, "orography": orography, "surface_flux": surface_flux, "send_list": send_list, "depth": depth, "ocean_state": ocean_state, "map_slot": map_slot, "map_weight": map_weight}


DRAG_SCALE = 1.0
SAT_SCALE = 0.1
BULK_SCALE = 0.2
TEND_SCALE = 8.0
WIND_PUSH = 0.1
HEAT_RATE = 0.2
SALT_RATE = 0.3
TIME_STEP = 0.6
GRAVITY = 1.0
BOTTOM_DRAG = 0.05
CORIOLIS_MAX = 0.2

def reference(wind_u, wind_v, buoyancy_freq, air_density, layer_mass, orography, surface_flux, send_list, depth, ocean_state, map_slot, map_weight):
    east_wind = wind_u.astype(jnp.float32)
    north_wind = wind_v.astype(jnp.float32)
    buoyancy = buoyancy_freq.astype(jnp.float32)
    density = air_density.astype(jnp.float32)
    thickness = layer_mass.astype(jnp.float32)
    surface_speed = jnp.sqrt(east_wind[0] * east_wind[0] + north_wind[0] * north_wind[0])
    dir_east = east_wind[0] / surface_speed
    dir_north = north_wind[0] / surface_speed
    base_stress = DRAG_SCALE * density[0] * buoyancy[0] * orography * orography * surface_speed
    speed_all = jnp.sqrt(east_wind * east_wind + north_wind * north_wind)
    saturated = SAT_SCALE * density * speed_all * speed_all * speed_all / buoyancy
    stress = jnp.minimum(base_stress[None], lax.cummin(saturated, axis=0))
    stress_below = jnp.concatenate([base_stress[None], stress[:-1]], axis=0)
    change = TEND_SCALE * (stress - stress_below) / thickness
    drag_tendency = jnp.stack([change * dir_east[None], change * dir_north[None]]).astype(jnp.bfloat16)
    bulk_drag = BULK_SCALE * density[0] * surface_speed
    stress_east = base_stress * dir_east + bulk_drag * east_wind[0]
    stress_north = base_stress * dir_north + bulk_drag * north_wind[0]
    fields = jnp.concatenate([stress_east[None], stress_north[None], surface_flux], axis=0)
    devices = N_COMP * N_SUB
    block_base = jnp.arange(devices, dtype=jnp.int32) * A_DEV
    columns = send_list + block_base[:, None, None]
    columns = jnp.transpose(columns, (1, 0, 2)).reshape(devices, devices * CAP)
    row_owner = jnp.arange(NOY, dtype=jnp.int32) // OY
    col_owner = jnp.arange(NOX, dtype=jnp.int32) // OX
    owner = row_owner[:, None] * N_SUB + col_owner[None, :]
    forcing = jnp.zeros((8, NOY, NOX), jnp.float32)
    for entry_idx in range(K):
        source_col = columns[owner, map_slot[entry_idx]]
        forcing = forcing + map_weight[entry_idx][None] * fields[:, source_col]
    push_east = WIND_PUSH * forcing[0] / depth
    push_north = WIND_PUSH * forcing[1] / depth
    sea_temp = ocean_state[3] + HEAT_RATE * (forcing[2] + forcing[3] + forcing[4] + forcing[5])
    sea_salt = ocean_state[4] - SALT_RATE * (forcing[6] - forcing[7])
    phase = 2.0 * math.pi * (jnp.arange(NOY, dtype=jnp.int32).astype(jnp.float32) + 0.5) / NOY
    coriolis = CORIOLIS_MAX * jnp.cos(phase)[:, None]
    height = ocean_state[0]
    vel_east = ocean_state[1]
    vel_north = ocean_state[2]
    for substep in range(SUBCYCLES):
        grad_east = (jnp.roll(height, -1, axis=1) - jnp.roll(height, 1, axis=1)) * 0.5
        grad_north = (jnp.roll(height, -1, axis=0) - jnp.roll(height, 1, axis=0)) * 0.5
        new_east = vel_east + TIME_STEP * (coriolis * vel_north - GRAVITY * grad_east + push_east - BOTTOM_DRAG * vel_east)
        new_north = vel_north + TIME_STEP * (-coriolis * vel_east - GRAVITY * grad_north + push_north - BOTTOM_DRAG * vel_north)
        flux_east = depth * new_east
        flux_north = depth * new_north
        divergence = (jnp.roll(flux_east, -1, axis=1) - jnp.roll(flux_east, 1, axis=1)) * 0.5 + (jnp.roll(flux_north, -1, axis=0) - jnp.roll(flux_north, 1, axis=0)) * 0.5
        height = height - TIME_STEP * divergence
        vel_east = new_east
        vel_north = new_north
    ocean_out = jnp.stack([height, vel_east, vel_north, sea_temp, sea_salt])
    return (drag_tendency, ocean_out)
```

```python
import functools
import math

import jax
import jax.numpy as jnp
from jax import lax
from jax.experimental import pallas as pl
from jax.experimental.pallas import tpu as pltpu
from jax.sharding import PartitionSpec as P

SUBCYCLES = 8

SAT_SCALE = 0.1
BULK_SCALE = 0.2
TEND_SCALE = 8.0
WIND_PUSH = 0.1
HEAT_RATE = 0.2
SALT_RATE = 0.3
TIME_STEP = 0.6
BOTTOM_DRAG = 0.05
CORIOLIS_MAX = 0.2

LANES = 128
HALO = 2 * SUBCYCLES
GUARD = 8
TOP = GUARD + HALO
MESH = pl.DeviceIdType.MESH


def lane_gather(values, idx):
    return jnp.take_along_axis(values, idx, axis=1, mode="promise_in_bounds")


def gather_row_tile(values, idx):
    halves = [
        lane_gather(values[:, at : at + LANES], idx[:, at : at + LANES])
        for at in range(0, values.shape[1], LANES)
    ]
    return jnp.concatenate(halves, axis=1)


def kernel(
    n_comp,
    n_sub,
    wind_u,
    wind_v,
    buoyancy_freq,
    air_density,
    layer_mass,
    orography,
    surface_flux,
    send_list,
    depth,
    ocean_state,
    map_slot,
    map_weight,
    drag_hbm,
    ocean_hbm,
    wu,
    wv,
    bf,
    ad,
    lm,
    oro,
    flux,
    sends,
    slots,
    weights,
    tracers,
    drag,
    surface,
    fields,
    outgoing,
    received,
    state,
    push,
    cor,
    flux_n,
    height_x,
    pack_state,
    halo_state,
    pack_push,
    halo_push,
    in_sem,
    out_sem,
    a2a_send,
    a2a_recv,
    st_send,
    st_recv,
    pu_send,
    pu_recv,
):
    devices = n_comp * n_sub
    comp = lax.axis_index("comp")
    sub = lax.axis_index("sub")
    me = comp * n_sub + sub
    rows_dev, cols_dev = depth.shape
    per = sends.shape[1]
    dpt = 8 // per
    tiles = devices // dpt
    bottom = TOP + rows_dev
    levels, columns = wu.shape

    barrier = pltpu.get_barrier_semaphore()

    def greet(k, carry):
        d = lax.rem(me + k, devices)
        pl.semaphore_signal(
            barrier, inc=1, device_id={"comp": d // n_sub, "sub": lax.rem(d, n_sub)}, device_id_type=MESH
        )
        return carry

    lax.fori_loop(1, devices, greet, 0)

    loads = []

    def load(src, dst):
        copy = pltpu.make_async_copy(src, dst, in_sem.at[len(loads)])
        copy.start()
        loads.append(copy)
        return copy

    first = [
        load(wind_u, wu),
        load(wind_v, wv),
        load(buoyancy_freq, bf),
        load(air_density, ad),
        load(orography, oro),
        load(surface_flux, flux),
    ]
    first += [
        load(send_list.at[0, :, pl.ds(j * cols_dev, cols_dev)], sends.at[:, j]) for j in range(per)
    ]
    second = [
        load(ocean_state.at[0:3], state.at[0:3, pl.ds(TOP, rows_dev), pl.ds(0, cols_dev)]),
        load(depth, state.at[3, pl.ds(TOP, rows_dev), pl.ds(0, cols_dev)]),
    ]
    third = [load(layer_mass, lm)]
    fourth = [
        load(ocean_state.at[3:5], tracers),
        load(map_slot, slots),
        load(map_weight, weights),
    ]

    for guard in (0, bottom + HALO):
        state[:, guard : guard + GUARD, :] = jnp.zeros((4, GUARD, state.shape[2]), jnp.float32)
        flux_n[guard : guard + GUARD, :] = jnp.zeros((GUARD, state.shape[2]), jnp.float32)

    for copy in first:
        copy.wait()
    east = wu[0:1, :].astype(jnp.float32)
    north = wv[0:1, :].astype(jnp.float32)
    dens = ad[0:1, :].astype(jnp.float32)
    buoy = bf[0:1, :].astype(jnp.float32)
    height_sd = oro[0:1, :]
    speed = jnp.sqrt(east * east + north * north)
    inverse = 1.0 / speed
    dir_east = east * inverse
    dir_north = north * inverse
    base = dens * buoy * height_sd * height_sd * speed
    bulk = BULK_SCALE * dens * speed
    surface[0:1, :] = base
    surface[1:2, :] = TEND_SCALE * dir_east
    surface[2:3, :] = TEND_SCALE * dir_north
    sources = [
        base * dir_east + bulk * east,
        base * dir_north + bulk * north,
        flux[0:1, :] + flux[1:2, :] + flux[2:3, :] + flux[3:4, :],
        flux[4:5, :] - flux[5:6, :],
    ]
    field_rows = columns // cols_dev
    for f in range(4):
        for r in range(field_rows):
            fields[f, r : r + 1, :] = sources[f][:, r * cols_dev : (r + 1) * cols_dev]

    pl.semaphore_wait(barrier, devices - 1)

    def a2a_copy(d):
        return pltpu.make_async_remote_copy(
            src_ref=outgoing.at[d],
            dst_ref=received.at[me],
            send_sem=a2a_send.at[d],
            recv_sem=a2a_recv.at[me],
            device_id={"comp": d // n_sub, "sub": lax.rem(d, n_sub)},
            device_id_type=MESH,
        )

    def a2a_arrival(s):
        return pltpu.make_async_remote_copy(
            src_ref=outgoing.at[s],
            dst_ref=received.at[s],
            send_sem=a2a_send.at[s],
            recv_sem=a2a_recv.at[s],
            device_id={"comp": s // n_sub, "sub": lax.rem(s, n_sub)},
            device_id_type=MESH,
        )

    def pick(i, carry):
        tile = lax.rem(me // dpt + 1 + i, tiles)
        base_row = pl.multiple_of(lax.rem(tile, field_rows // 8) * 8, 8)
        idx = jnp.concatenate([sends[tile * dpt + j] for j in range(dpt)], axis=0) & (LANES - 1)
        for f in range(4):
            got = gather_row_tile(fields[f, pl.ds(base_row, 8), :], idx)
            for j in range(dpt):
                outgoing[tile * dpt + j, f] = got[j * per : (j + 1) * per]
        for j in range(dpt):
            d = tile * dpt + j

            @pl.when(d != me)
            def _():
                a2a_copy(d).start()

            @pl.when(d == me)
            def _():
                received[d] = outgoing[d]

        return carry

    lax.fori_loop(0, tiles, pick, 0)

    def halo_copies(cells, pack, halo, send_sem, recv_sem):
        up = lax.rem(comp + n_comp - 1, n_comp)
        down = lax.rem(comp + 1, n_comp)
        right = lax.rem(sub + 1, n_sub)
        left = lax.rem(sub + n_sub - 1, n_sub)
        wide = pl.ds(0, cols_dev)
        plan = [
            (
                cells.at[:, pl.ds(bottom - HALO, HALO), wide],
                cells.at[:, pl.ds(GUARD, HALO), wide],
                (down, sub),
            ),
            (
                cells.at[:, pl.ds(TOP, HALO), wide],
                cells.at[:, pl.ds(bottom, HALO), wide],
                (up, sub),
            ),
        ]
        for side, there in ((0, right), (1, left)):
            plan += [
                (pack.at[side], halo.at[side, pl.ds(HALO, rows_dev)], (comp, there)),
                (
                    pack.at[side, pl.ds(rows_dev - HALO, HALO)],
                    halo.at[side, pl.ds(0, HALO)],
                    (down, there),
                ),
                (
                    pack.at[side, pl.ds(0, HALO)],
                    halo.at[side, pl.ds(HALO + rows_dev, HALO)],
                    (up, there),
                ),
            ]
        return [
            pltpu.make_async_remote_copy(
                src_ref=src,
                dst_ref=dst,
                send_sem=send_sem.at[i],
                recv_sem=recv_sem.at[i],
                device_id={"comp": target[0], "sub": target[1]},
                device_id_type=MESH,
            )
            for i, (src, dst, target) in enumerate(plan)
        ]

    lane = lax.broadcasted_iota(jnp.int32, (rows_dev, LANES), 1)
    lane_halo = lax.broadcasted_iota(jnp.int32, (rows_dev + 2 * HALO, LANES), 1)

    def pack_edges(cells, count, pack):
        right_edge = cells[0, TOP:bottom, cols_dev - LANES : cols_dev]
        left_edge = cells[0, TOP:bottom, 0:LANES]
        for k in range(1, count):
            tile = cells[k, TOP:bottom, cols_dev - LANES : cols_dev]
            right_edge = jnp.where(
                lane < LANES - k * HALO, pltpu.roll(tile, LANES - k * HALO, 1), right_edge
            )
            tile = cells[k, TOP:bottom, 0:LANES]
            left_edge = jnp.where(lane >= k * HALO, pltpu.roll(tile, k * HALO, 1), left_edge)
        pack[0] = right_edge
        pack[1] = left_edge

    def unpack_edges(cells, count, halo):
        from_left = halo[0]
        from_right = halo[1]
        for k in range(count):
            left_k = pltpu.roll(from_left, k * HALO, 1) if k else from_left
            right_k = pltpu.roll(from_right, LANES - k * HALO, 1) if k else from_right
            cells[k, GUARD : bottom + HALO, cols_dev : cols_dev + LANES] = jnp.where(
                lane_halo < LANES // 2, right_k, left_k
            )

    for copy in second:
        copy.wait()
    pack_edges(state, 4, pack_state)
    state_copies = halo_copies(state, pack_state, halo_state, st_send, st_recv)
    for copy in state_copies:
        copy.start()

    total_rows = cor.shape[0]
    row_global = comp * rows_dev - TOP + lax.broadcasted_iota(jnp.int32, cor.shape, 0)
    phase = 2.0 * math.pi * (row_global.astype(jnp.float32) + 0.5) / (rows_dev * n_comp)
    cor[...] = (TIME_STEP * CORIOLIS_MAX) * jnp.cos(phase)

    for copy in third:
        copy.wait()
    width = 2 * LANES
    row8 = lax.broadcasted_iota(jnp.int32, (8, width), 0)

    def drag_chunk(c, carry):
        at = pl.ds(pl.multiple_of(c * width, width), width)
        u = wu[:, at].astype(jnp.float32)
        v = wv[:, at].astype(jnp.float32)
        sq = u * u + v * v
        sat = (
            SAT_SCALE
            * ad[:, at].astype(jnp.float32)
            * (sq * sq * lax.rsqrt(sq))
            / bf[:, at].astype(jnp.float32)
        )
        inv_mass = 1.0 / lm[:, at].astype(jnp.float32)
        above = jnp.broadcast_to(surface[0:1, at], (8, width))
        dir_e = jnp.broadcast_to(surface[1:2, at], (8, width))
        dir_n = jnp.broadcast_to(surface[2:3, at], (8, width))
        out_e = []
        out_n = []
        for lev in range(0, levels, 8):
            low = jnp.minimum(sat[lev : lev + 8], above)
            for shift in (1, 2, 4):
                low = jnp.minimum(low, jnp.where(row8 >= shift, pltpu.roll(low, shift, 0), low))
            below = jnp.where(row8 >= 1, pltpu.roll(low, 1, 0), above)
            change = (low - below) * inv_mass[lev : lev + 8]
            out_e.append(change * dir_e)
            out_n.append(change * dir_n)
            above = jnp.broadcast_to(low[7:8], (8, width))
        drag[0, :, at] = jnp.concatenate(out_e, axis=0).astype(jnp.bfloat16)
        drag[1, :, at] = jnp.concatenate(out_n, axis=0).astype(jnp.bfloat16)
        return carry

    lax.fori_loop(0, columns // width, drag_chunk, 0)
    drag_store = pltpu.make_async_copy(drag, drag_hbm, out_sem.at[0])
    drag_store.start()

    for copy in fourth:
        copy.wait()

    def spread(i, carry):
        tile = lax.rem(me // dpt + tiles - i, tiles)
        for j in range(dpt):
            s = tile * dpt + j

            @pl.when(s != me)
            def _():
                a2a_arrival(s).wait_recv()

        rows = pl.ds(pl.multiple_of(tile * 8, 8), 8)
        rows_in = pl.ds(pl.multiple_of(TOP + tile * 8, 8), 8)
        wide = pl.ds(0, cols_dev)
        idx = [slots[k, rows, :] & (LANES - 1) for k in range(slots.shape[0])]
        wgt = [weights[k, rows, :] for k in range(slots.shape[0])]
        forcing = []
        for f in range(4):
            values = jnp.concatenate([received[tile * dpt + j, f] for j in range(dpt)], axis=0)
            terms = [w * gather_row_tile(values, x) for w, x in zip(wgt, idx)]
            forcing.append(sum(terms[1:], terms[0]))
        scale = (TIME_STEP * WIND_PUSH) / state[3, rows_in, wide]
        push[0, rows_in, wide] = forcing[0] * scale
        push[1, rows_in, wide] = forcing[1] * scale
        tracers[0, rows, :] = tracers[0, rows, :] + HEAT_RATE * forcing[2]
        tracers[1, rows, :] = tracers[1, rows, :] - SALT_RATE * forcing[3]
        return carry

    lax.fori_loop(0, tiles, spread, 0)

    pack_edges(push, 2, pack_push)
    push_copies = halo_copies(push, pack_push, halo_push, pu_send, pu_recv)
    for copy in push_copies:
        copy.start()
    tracer_store = pltpu.make_async_copy(tracers, ocean_hbm.at[3:5], out_sem.at[1])
    tracer_store.start()
    for copy in state_copies:
        copy.wait_recv()
    unpack_edges(state, 4, halo_state)
    for copy in state_copies:
        copy.wait_send()
    for copy in push_copies:
        copy.wait()
    unpack_edges(push, 2, halo_push)

    span = state.shape[2]
    keep = 1.0 - TIME_STEP * BOTTOM_DRAG
    half = 0.5 * TIME_STEP
    chunk = 16
    copies = span // LANES

    def diff_east(a):
        return pltpu.roll(a, span - 1, 1) - pltpu.roll(a, 1, 1)

    def step(n, carry):
        for a in range(GUARD, bottom + HALO, chunk):
            h = state[0, a : a + chunk, :]
            u = state[1, a : a + chunk, :]
            v = state[2, a : a + chunk, :]
            d = state[3, a : a + chunk, :]
            turn = jnp.concatenate([cor[a : a + chunk, :]] * copies, axis=1)
            grad_n = state[0, a + 1 : a + chunk + 1, :] - state[0, a - 1 : a + chunk - 1, :]
            new_u = keep * u + turn * v - half * diff_east(h) + push[0, a : a + chunk, :]
            new_v = keep * v - turn * u - half * grad_n + push[1, a : a + chunk, :]
            state[1, a : a + chunk, :] = new_u
            state[2, a : a + chunk, :] = new_v
            flux_n[a : a + chunk, :] = d * new_v
            height_x[a : a + chunk, :] = h - half * diff_east(d * new_u)
        for a in range(GUARD, bottom + HALO, chunk):
            div_n = flux_n[a + 1 : a + chunk + 1, :] - flux_n[a - 1 : a + chunk - 1, :]
            state[0, a : a + chunk, :] = height_x[a : a + chunk, :] - half * div_n
        return carry

    lax.fori_loop(0, SUBCYCLES, step, 0)
    ocean_store = pltpu.make_async_copy(
        state.at[0:3, pl.ds(TOP, rows_dev), pl.ds(0, cols_dev)], ocean_hbm.at[0:3], out_sem.at[2]
    )
    ocean_store.start()

    def drain(k, carry):
        a2a_copy(lax.rem(me + k, devices)).wait_send()
        return carry

    lax.fori_loop(1, devices, drain, 0)
    drag_store.wait()
    tracer_store.wait()
    ocean_store.wait()


def shards(n_comp, n_sub, *args):
    wind_u, orography, surface_flux, send_list = args[0], args[5], args[6], args[7]
    depth, ocean_state, map_slot, map_weight = args[8:12]
    devices = n_comp * n_sub
    levels, columns = wind_u.shape
    rows_dev, cols_dev = depth.shape
    entries = map_slot.shape[0]
    cap = send_list.shape[2]
    per = cap // cols_dev
    total_rows = rows_dev + 2 * TOP
    span = cols_dev + LANES
    halo_rows = rows_dev + 2 * HALO
    f32 = jnp.float32
    air = pltpu.VMEM((levels, columns), jnp.bfloat16)
    args = args[:5] + (orography.reshape(1, -1),) + args[6:]
    dma = pltpu.SemaphoreType.DMA
    return pl.pallas_call(
        functools.partial(kernel, n_comp, n_sub),
        out_shape=(
            jax.ShapeDtypeStruct((2, levels, columns), jnp.bfloat16),
            jax.ShapeDtypeStruct(ocean_state.shape, f32),
        ),
        in_specs=[pl.BlockSpec(memory_space=pl.ANY)] * 12,
        out_specs=[pl.BlockSpec(memory_space=pl.ANY)] * 2,
        scratch_shapes=[
            air,
            air,
            air,
            air,
            air,
            pltpu.VMEM((1, columns), f32),
            pltpu.VMEM(surface_flux.shape, f32),
            pltpu.VMEM((devices, per, cols_dev), jnp.int32),
            pltpu.VMEM((entries, rows_dev, cols_dev), jnp.int32),
            pltpu.VMEM((entries, rows_dev, cols_dev), f32),
            pltpu.VMEM((2, rows_dev, cols_dev), f32),
            pltpu.VMEM((2, levels, columns), jnp.bfloat16),
            pltpu.VMEM((8, columns), f32),
            pltpu.VMEM((4, columns // cols_dev, cols_dev), f32),
            pltpu.VMEM((devices, 4, per, cols_dev), f32),
            pltpu.VMEM((devices, 4, per, cols_dev), f32),
            pltpu.VMEM((4, total_rows, span), f32),
            pltpu.VMEM((2, total_rows, span), f32),
            pltpu.VMEM((total_rows, LANES), f32),
            pltpu.VMEM((total_rows, span), f32),
            pltpu.VMEM((total_rows, span), f32),
            pltpu.VMEM((2, rows_dev, LANES), f32),
            pltpu.VMEM((2, halo_rows, LANES), f32),
            pltpu.VMEM((2, rows_dev, LANES), f32),
            pltpu.VMEM((2, halo_rows, LANES), f32),
            dma((12 + per,)),
            dma((3,)),
            dma((devices,)),
            dma((devices,)),
            dma((8,)),
            dma((8,)),
            dma((8,)),
            dma((8,)),
        ],
        compiler_params=pltpu.CompilerParams(
            collective_id=0, has_side_effects=True, vmem_limit_bytes=40 * 1024 * 1024
        ),
    )(*args)


def solution(mesh):
    return jax.shard_map(
        functools.partial(shards, mesh.shape["comp"], mesh.shape["sub"]),
        mesh=mesh,
        in_specs=(
            P(None, ("group", "comp", "sub")),
            P(None, ("group", "comp", "sub")),
            P(None, ("group", "comp", "sub")),
            P(None, ("group", "comp", "sub")),
            P(None, ("group", "comp", "sub")),
            P(("comp", "sub")),
            P(None, ("group", "comp", "sub")),
            P(("comp", "sub"), None, None),
            P("comp", "sub"),
            P(None, ("group", "comp"), "sub"),
            P(None, "comp", "sub"),
            P(None, "comp", "sub"),
        ),
        out_specs=(P(None, None, ("group", "comp", "sub")), P(None, ("group", "comp"), "sub")),
        check_vma=False,
    )
```

```python
import functools
import math

import jax
import jax.numpy as jnp
from jax import lax
from jax.experimental import pallas as pl
from jax.experimental.pallas import tpu as pltpu
from jax.sharding import PartitionSpec as P

SUBCYCLES = 8

SAT_SCALE = 0.1
BULK_SCALE = 0.2
TEND_SCALE = 8.0
WIND_PUSH = 0.1
HEAT_RATE = 0.2
SALT_RATE = 0.3
TIME_STEP = 0.6
BOTTOM_DRAG = 0.05
CORIOLIS_MAX = 0.2

LANES = 128
HALO = 2 * SUBCYCLES
GUARD = 8
TOP = GUARD + HALO
MESH = pl.DeviceIdType.MESH


def lane_gather(values, idx):
    return jnp.take_along_axis(values, idx, axis=1, mode="promise_in_bounds")


def gather_row_tile(values, idx):
    halves = [
        lane_gather(values[:, at : at + LANES], idx[:, at : at + LANES])
        for at in range(0, values.shape[1], LANES)
    ]
    return jnp.concatenate(halves, axis=1)


def kernel(
    n_comp,
    n_sub,
    wind_u,
    wind_v,
    buoyancy_freq,
    air_density,
    layer_mass,
    orography,
    surface_flux,
    send_list,
    depth,
    ocean_state,
    map_slot,
    map_weight,
    drag_hbm,
    ocean_hbm,
    wu,
    wv,
    bf,
    ad,
    lm,
    oro,
    flux,
    sends,
    slots,
    weights,
    tracers,
    drag,
    surface,
    fields,
    outgoing,
    received,
    state,
    push,
    cor,
    flux_n,
    height_x,
    pack_state,
    halo_state,
    pack_push,
    halo_push,
    in_sem,
    out_sem,
    a2a_send,
    a2a_recv,
    st_send,
    st_recv,
    pu_send,
    pu_recv,
):
    devices = n_comp * n_sub
    comp = lax.axis_index("comp")
    sub = lax.axis_index("sub")
    me = comp * n_sub + sub
    rows_dev, cols_dev = depth.shape
    per = sends.shape[1]
    dpt = 8 // per
    tiles = devices // dpt
    bottom = TOP + rows_dev
    levels, columns = wu.shape

    barrier = pltpu.get_barrier_semaphore()

    def greet(k, carry):
        d = lax.rem(me + k, devices)
        pl.semaphore_signal(
            barrier, inc=1, device_id={"comp": d // n_sub, "sub": lax.rem(d, n_sub)}, device_id_type=MESH
        )
        return carry

    lax.fori_loop(1, devices, greet, 0)

    loads = []

    def load(src, dst):
        copy = pltpu.make_async_copy(src, dst, in_sem.at[len(loads)])
        copy.start()
        loads.append(copy)
        return copy

    second = [
        load(ocean_state.at[0:3], state.at[0:3, pl.ds(TOP, rows_dev), pl.ds(0, cols_dev)]),
        load(depth, state.at[3, pl.ds(TOP, rows_dev), pl.ds(0, cols_dev)]),
    ]
    first = [
        load(wind_u, wu),
        load(wind_v, wv),
        load(buoyancy_freq, bf),
        load(air_density, ad),
        load(orography, oro),
        load(surface_flux, flux),
    ]
    first += [
        load(send_list.at[0, :, pl.ds(j * cols_dev, cols_dev)], sends.at[:, j]) for j in range(per)
    ]
    third = [load(layer_mass, lm)]
    fourth = [
        load(ocean_state.at[3:5], tracers),
        load(map_slot, slots),
        load(map_weight, weights),
    ]

    for guard in (0, bottom + HALO):
        state[:, guard : guard + GUARD, :] = jnp.zeros((4, GUARD, state.shape[2]), jnp.float32)
        flux_n[guard : guard + GUARD, :] = jnp.zeros((GUARD, state.shape[2]), jnp.float32)

    def halo_copies(cells, pack, halo, send_sem, recv_sem):
        up = lax.rem(comp + n_comp - 1, n_comp)
        down = lax.rem(comp + 1, n_comp)
        right = lax.rem(sub + 1, n_sub)
        left = lax.rem(sub + n_sub - 1, n_sub)
        wide = pl.ds(0, cols_dev)
        plan = [
            (
                cells.at[:, pl.ds(bottom - HALO, HALO), wide],
                cells.at[:, pl.ds(GUARD, HALO), wide],
                (down, sub),
            ),
            (
                cells.at[:, pl.ds(TOP, HALO), wide],
                cells.at[:, pl.ds(bottom, HALO), wide],
                (up, sub),
            ),
        ]
        for side, there in ((0, right), (1, left)):
            plan += [
                (pack.at[side], halo.at[side, pl.ds(HALO, rows_dev)], (comp, there)),
                (
                    pack.at[side, pl.ds(rows_dev - HALO, HALO)],
                    halo.at[side, pl.ds(0, HALO)],
                    (down, there),
                ),
                (
                    pack.at[side, pl.ds(0, HALO)],
                    halo.at[side, pl.ds(HALO + rows_dev, HALO)],
                    (up, there),
                ),
            ]
        return [
            pltpu.make_async_remote_copy(
                src_ref=src,
                dst_ref=dst,
                send_sem=send_sem.at[i],
                recv_sem=recv_sem.at[i],
                device_id={"comp": target[0], "sub": target[1]},
                device_id_type=MESH,
            )
            for i, (src, dst, target) in enumerate(plan)
        ]

    lane_halo = lax.broadcasted_iota(jnp.int32, (rows_dev + 2 * HALO, LANES), 1)

    def pack_edges(cells, count, pack, begin, end):
        lane = lax.broadcasted_iota(jnp.int32, (end - begin, LANES), 1)
        rows = slice(TOP + begin, TOP + end)
        right_edge = cells[0, rows, cols_dev - LANES : cols_dev]
        left_edge = cells[0, rows, 0:LANES]
        for k in range(1, count):
            tile = cells[k, rows, cols_dev - LANES : cols_dev]
            right_edge = jnp.where(
                lane < LANES - k * HALO, pltpu.roll(tile, LANES - k * HALO, 1), right_edge
            )
            tile = cells[k, rows, 0:LANES]
            left_edge = jnp.where(lane >= k * HALO, pltpu.roll(tile, k * HALO, 1), left_edge)
        pack[0, begin:end] = right_edge
        pack[1, begin:end] = left_edge

    def unpack_edges(cells, count, halo):
        from_left = halo[0]
        from_right = halo[1]
        for k in range(count):
            left_k = pltpu.roll(from_left, k * HALO, 1) if k else from_left
            right_k = pltpu.roll(from_right, LANES - k * HALO, 1) if k else from_right
            cells[k, GUARD : bottom + HALO, cols_dev : cols_dev + LANES] = jnp.where(
                lane_halo < LANES // 2, right_k, left_k
            )

    for copy in second:
        copy.wait()
    pack_edges(state, 4, pack_state, 0, rows_dev)
    state_copies = halo_copies(state, pack_state, halo_state, st_send, st_recv)
    pl.semaphore_wait(barrier, devices - 1)
    for copy in state_copies:
        copy.start()

    for copy in first:
        copy.wait()
    east = wu[0:1, :].astype(jnp.float32)
    north = wv[0:1, :].astype(jnp.float32)
    dens = ad[0:1, :].astype(jnp.float32)
    buoy = bf[0:1, :].astype(jnp.float32)
    height_sd = oro[0:1, :]
    speed = jnp.sqrt(east * east + north * north)
    inverse = 1.0 / speed
    dir_east = east * inverse
    dir_north = north * inverse
    base = dens * buoy * height_sd * height_sd * speed
    bulk = BULK_SCALE * dens * speed
    surface[0:1, :] = base
    surface[1:2, :] = TEND_SCALE * dir_east
    surface[2:3, :] = TEND_SCALE * dir_north
    sources = [
        base * dir_east + bulk * east,
        base * dir_north + bulk * north,
        flux[0:1, :] + flux[1:2, :] + flux[2:3, :] + flux[3:4, :],
        flux[4:5, :] - flux[5:6, :],
    ]
    field_rows = columns // cols_dev
    for f in range(4):
        for r in range(field_rows):
            fields[f, r : r + 1, :] = sources[f][:, r * cols_dev : (r + 1) * cols_dev]

    def a2a_copy(d):
        return pltpu.make_async_remote_copy(
            src_ref=outgoing.at[d],
            dst_ref=received.at[me],
            send_sem=a2a_send.at[d],
            recv_sem=a2a_recv.at[me],
            device_id={"comp": d // n_sub, "sub": lax.rem(d, n_sub)},
            device_id_type=MESH,
        )

    def a2a_arrival(s):
        return pltpu.make_async_remote_copy(
            src_ref=outgoing.at[s],
            dst_ref=received.at[s],
            send_sem=a2a_send.at[s],
            recv_sem=a2a_recv.at[s],
            device_id={"comp": s // n_sub, "sub": lax.rem(s, n_sub)},
            device_id_type=MESH,
        )

    def pick(i, carry):
        tile = lax.rem(me // dpt + 1 + i, tiles)
        base_row = pl.multiple_of(lax.rem(tile, field_rows // 8) * 8, 8)
        idx = jnp.concatenate([sends[tile * dpt + j] for j in range(dpt)], axis=0) & (LANES - 1)
        for f in range(4):
            got = gather_row_tile(fields[f, pl.ds(base_row, 8), :], idx)
            for j in range(dpt):
                outgoing[tile * dpt + j, f] = got[j * per : (j + 1) * per]
        for j in range(dpt):
            d = tile * dpt + j

            @pl.when(d != me)
            def _():
                a2a_copy(d).start()

            @pl.when(d == me)
            def _():
                received[d] = outgoing[d]

        return carry

    lax.fori_loop(0, tiles, pick, 0)

    total_rows = cor.shape[0]
    row_global = comp * rows_dev - TOP + lax.broadcasted_iota(jnp.int32, cor.shape, 0)
    phase = 2.0 * math.pi * (row_global.astype(jnp.float32) + 0.5) / (rows_dev * n_comp)
    cor[...] = (TIME_STEP * CORIOLIS_MAX) * jnp.cos(phase)

    for copy in third:
        copy.wait()
    width = 2 * LANES
    row8 = lax.broadcasted_iota(jnp.int32, (8, width), 0)

    def drag_chunk(c, carry):
        at = pl.ds(pl.multiple_of(c * width, width), width)
        u = wu[:, at].astype(jnp.float32)
        v = wv[:, at].astype(jnp.float32)
        sq = u * u + v * v
        sat = (
            SAT_SCALE
            * ad[:, at].astype(jnp.float32)
            * (sq * sq * lax.rsqrt(sq))
            / bf[:, at].astype(jnp.float32)
        )
        inv_mass = 1.0 / lm[:, at].astype(jnp.float32)
        above = jnp.broadcast_to(surface[0:1, at], (8, width))
        dir_e = jnp.broadcast_to(surface[1:2, at], (8, width))
        dir_n = jnp.broadcast_to(surface[2:3, at], (8, width))
        out_e = []
        out_n = []
        for lev in range(0, levels, 8):
            low = jnp.minimum(sat[lev : lev + 8], above)
            for shift in (1, 2, 4):
                low = jnp.minimum(low, jnp.where(row8 >= shift, pltpu.roll(low, shift, 0), low))
            below = jnp.where(row8 >= 1, pltpu.roll(low, 1, 0), above)
            change = (low - below) * inv_mass[lev : lev + 8]
            out_e.append(change * dir_e)
            out_n.append(change * dir_n)
            above = jnp.broadcast_to(low[7:8], (8, width))
        drag[0, :, at] = jnp.concatenate(out_e, axis=0).astype(jnp.bfloat16)
        drag[1, :, at] = jnp.concatenate(out_n, axis=0).astype(jnp.bfloat16)
        return carry

    lax.fori_loop(0, columns // width, drag_chunk, 0)
    drag_store = pltpu.make_async_copy(drag, drag_hbm, out_sem.at[0])
    drag_store.start()

    for copy in fourth:
        copy.wait()

    def spread(tile):
        for j in range(dpt):
            s = tile * dpt + j

            @pl.when(s != me)
            def _():
                a2a_arrival(s).wait_recv()

        rows = pl.ds(pl.multiple_of(tile * 8, 8), 8)
        rows_in = pl.ds(pl.multiple_of(TOP + tile * 8, 8), 8)
        wide = pl.ds(0, cols_dev)
        idx = [slots[k, rows, :] & (LANES - 1) for k in range(slots.shape[0])]
        wgt = [weights[k, rows, :] for k in range(slots.shape[0])]
        forcing = []
        for f in range(4):
            values = jnp.concatenate([received[tile * dpt + j, f] for j in range(dpt)], axis=0)
            terms = [w * gather_row_tile(values, x) for w, x in zip(wgt, idx)]
            forcing.append(sum(terms[1:], terms[0]))
        scale = (TIME_STEP * WIND_PUSH) / state[3, rows_in, wide]
        push[0, rows_in, wide] = forcing[0] * scale
        push[1, rows_in, wide] = forcing[1] * scale
        tracers[0, rows, :] = tracers[0, rows, :] + HEAT_RATE * forcing[2]
        tracers[1, rows, :] = tracers[1, rows, :] - SALT_RATE * forcing[3]

    edge = HALO // 8
    inner = tiles - 2 * edge

    def spread_edge(i, carry):
        spread(jnp.where(i < edge, i, i + inner))
        return carry

    def spread_inner(i, carry):
        spread(edge + lax.rem(me // dpt + 2 * inner - i, inner))
        return carry

    push_copies = halo_copies(push, pack_push, halo_push, pu_send, pu_recv)
    lax.fori_loop(0, 2 * edge, spread_edge, 0)
    pack_edges(push, 2, pack_push, 0, HALO)
    pack_edges(push, 2, pack_push, rows_dev - HALO, rows_dev)
    for i in (0, 1, 3, 4, 6, 7):
        push_copies[i].start()
    lax.fori_loop(0, inner, spread_inner, 0)
    pack_edges(push, 2, pack_push, HALO, rows_dev - HALO)
    for i in (2, 5):
        push_copies[i].start()
    tracer_store = pltpu.make_async_copy(tracers, ocean_hbm.at[3:5], out_sem.at[1])
    tracer_store.start()
    for copy in state_copies:
        copy.wait_recv()
    unpack_edges(state, 4, halo_state)
    for copy in state_copies:
        copy.wait_send()
    for copy in push_copies:
        copy.wait()
    unpack_edges(push, 2, halo_push)

    span = state.shape[2]
    keep = 1.0 - TIME_STEP * BOTTOM_DRAG
    half = 0.5 * TIME_STEP
    chunk = 16
    copies = span // LANES

    def diff_east(a):
        return pltpu.roll(a, span - 1, 1) - pltpu.roll(a, 1, 1)

    def step(n, carry):
        for a in range(GUARD, bottom + HALO, chunk):
            h = state[0, a : a + chunk, :]
            u = state[1, a : a + chunk, :]
            v = state[2, a : a + chunk, :]
            d = state[3, a : a + chunk, :]
            turn = jnp.concatenate([cor[a : a + chunk, :]] * copies, axis=1)
            grad_n = state[0, a + 1 : a + chunk + 1, :] - state[0, a - 1 : a + chunk - 1, :]
            new_u = keep * u + turn * v - half * diff_east(h) + push[0, a : a + chunk, :]
            new_v = keep * v - turn * u - half * grad_n + push[1, a : a + chunk, :]
            state[1, a : a + chunk, :] = new_u
            state[2, a : a + chunk, :] = new_v
            flux_n[a : a + chunk, :] = d * new_v
            height_x[a : a + chunk, :] = h - half * diff_east(d * new_u)
        for a in range(GUARD, bottom + HALO, chunk):
            div_n = flux_n[a + 1 : a + chunk + 1, :] - flux_n[a - 1 : a + chunk - 1, :]
            state[0, a : a + chunk, :] = height_x[a : a + chunk, :] - half * div_n
        return carry

    lax.fori_loop(0, SUBCYCLES, step, 0)
    ocean_store = pltpu.make_async_copy(
        state.at[0:3, pl.ds(TOP, rows_dev), pl.ds(0, cols_dev)], ocean_hbm.at[0:3], out_sem.at[2]
    )
    ocean_store.start()

    def drain(k, carry):
        a2a_copy(lax.rem(me + k, devices)).wait_send()
        return carry

    lax.fori_loop(1, devices, drain, 0)
    drag_store.wait()
    tracer_store.wait()
    ocean_store.wait()


def shards(n_comp, n_sub, *args):
    wind_u, orography, surface_flux, send_list = args[0], args[5], args[6], args[7]
    depth, ocean_state, map_slot, map_weight = args[8:12]
    devices = n_comp * n_sub
    levels, columns = wind_u.shape
    rows_dev, cols_dev = depth.shape
    entries = map_slot.shape[0]
    cap = send_list.shape[2]
    per = cap // cols_dev
    total_rows = rows_dev + 2 * TOP
    span = cols_dev + LANES
    halo_rows = rows_dev + 2 * HALO
    f32 = jnp.float32
    air = pltpu.VMEM((levels, columns), jnp.bfloat16)
    args = args[:5] + (orography.reshape(1, -1),) + args[6:]
    dma = pltpu.SemaphoreType.DMA
    return pl.pallas_call(
        functools.partial(kernel, n_comp, n_sub),
        out_shape=(
            pltpu.VMEM((2, levels, columns), jnp.bfloat16),
            jax.ShapeDtypeStruct(ocean_state.shape, f32),
        ),
        in_specs=[pl.BlockSpec(memory_space=pltpu.HBM)] * 12,
        out_specs=[pl.BlockSpec(memory_space=pltpu.HBM)] * 2,
        scratch_shapes=[
            air,
            air,
            air,
            air,
            air,
            pltpu.VMEM((1, columns), f32),
            pltpu.VMEM(surface_flux.shape, f32),
            pltpu.VMEM((devices, per, cols_dev), jnp.int32),
            pltpu.VMEM((entries, rows_dev, cols_dev), jnp.int32),
            pltpu.VMEM((entries, rows_dev, cols_dev), f32),
            pltpu.VMEM((2, rows_dev, cols_dev), f32),
            pltpu.VMEM((2, levels, columns), jnp.bfloat16),
            pltpu.VMEM((8, columns), f32),
            pltpu.VMEM((4, columns // cols_dev, cols_dev), f32),
            pltpu.VMEM((devices, 4, per, cols_dev), f32),
            pltpu.VMEM((devices, 4, per, cols_dev), f32),
            pltpu.VMEM((4, total_rows, span), f32),
            pltpu.VMEM((2, total_rows, span), f32),
            pltpu.VMEM((total_rows, LANES), f32),
            pltpu.VMEM((total_rows, span), f32),
            pltpu.VMEM((total_rows, span), f32),
            pltpu.VMEM((2, rows_dev, LANES), f32),
            pltpu.VMEM((2, halo_rows, LANES), f32),
            pltpu.VMEM((2, rows_dev, LANES), f32),
            pltpu.VMEM((2, halo_rows, LANES), f32),
            dma((12 + per,)),
            dma((3,)),
            dma((devices,)),
            dma((devices,)),
            dma((8,)),
            dma((8,)),
            dma((8,)),
            dma((8,)),
        ],
        compiler_params=pltpu.CompilerParams(
            collective_id=0, has_side_effects=True, vmem_limit_bytes=58 * 1024 * 1024
        ),
    )(*args)


def solution(mesh):
    return jax.shard_map(
        functools.partial(shards, mesh.shape["comp"], mesh.shape["sub"]),
        mesh=mesh,
        in_specs=(
            P(None, ("group", "comp", "sub")),
            P(None, ("group", "comp", "sub")),
            P(None, ("group", "comp", "sub")),
            P(None, ("group", "comp", "sub")),
            P(None, ("group", "comp", "sub")),
            P(("comp", "sub")),
            P(None, ("group", "comp", "sub")),
            P(("comp", "sub"), None, None),
            P("comp", "sub"),
            P(None, ("group", "comp"), "sub"),
            P(None, "comp", "sub"),
            P(None, "comp", "sub"),
        ),
        out_specs=(P(None, None, ("group", "comp", "sub")), P(None, ("group", "comp"), "sub")),
        check_vma=False,
    )
```

```python
import functools
import math

import jax
import jax.numpy as jnp
from jax import lax
from jax.experimental import pallas as pl
from jax.experimental.pallas import tpu as pltpu
from jax.sharding import PartitionSpec as P

SUBCYCLES = 8

SAT_SCALE = 0.1
BULK_SCALE = 0.2
TEND_SCALE = 8.0
WIND_PUSH = 0.1
HEAT_RATE = 0.2
SALT_RATE = 0.3
TIME_STEP = 0.6
BOTTOM_DRAG = 0.05
CORIOLIS_MAX = 0.2

LANES = 128
HALO = 2 * SUBCYCLES
GUARD = 8
TOP = GUARD + HALO
MESH = pl.DeviceIdType.MESH


def lane_gather(values, idx):
    return jnp.take_along_axis(values, idx, axis=1, mode="promise_in_bounds")


def gather_row_tile(values, idx):
    halves = [
        lane_gather(values[:, at : at + LANES], idx[:, at : at + LANES])
        for at in range(0, values.shape[1], LANES)
    ]
    return jnp.concatenate(halves, axis=1)


def kernel(
    n_comp,
    n_sub,
    wind_u,
    wind_v,
    buoyancy_freq,
    air_density,
    layer_mass,
    orography,
    surface_flux,
    send_list,
    depth,
    ocean_state,
    map_slot,
    map_weight,
    drag_hbm,
    ocean_hbm,
    wu,
    wv,
    bf,
    ad,
    lm,
    oro,
    flux,
    sends,
    slots,
    weights,
    tracers,
    drag,
    surface,
    fields,
    tables,
    stage,
    received,
    state,
    push,
    cor,
    flux_n,
    height_x,
    pack_state,
    halo_state,
    pack_push,
    halo_push,
    in_sem,
    out_sem,
    ix_send,
    ix_recv,
    z_send,
    z_recv,
    a2a_send,
    a2a_recv,
    st_send,
    st_recv,
    pu_send,
    pu_recv,
):
    devices = n_comp * n_sub
    comp = lax.axis_index("comp")
    sub = lax.axis_index("sub")
    me = comp * n_sub + sub
    rows_dev, cols_dev = depth.shape
    per = sends.shape[1]
    dpt = 8 // per
    tiles = devices // dpt
    bottom = TOP + rows_dev
    levels, columns = wu.shape

    barrier = pltpu.get_barrier_semaphore()

    def greet(k, carry):
        d = lax.rem(me + k, devices)
        pl.semaphore_signal(
            barrier, inc=1, device_id={"comp": d // n_sub, "sub": lax.rem(d, n_sub)}, device_id_type=MESH
        )
        return carry

    lax.fori_loop(1, devices, greet, 0)

    loads = []

    def load(src, dst):
        copy = pltpu.make_async_copy(src, dst, in_sem.at[len(loads)])
        copy.start()
        loads.append(copy)
        return copy

    second = [
        load(ocean_state.at[0:3], state.at[0:3, pl.ds(TOP, rows_dev), pl.ds(0, cols_dev)]),
        load(depth, state.at[3, pl.ds(TOP, rows_dev), pl.ds(0, cols_dev)]),
    ]
    first = [
        load(wind_u, wu),
        load(wind_v, wv),
        load(buoyancy_freq, bf),
        load(air_density, ad),
        load(orography, oro),
        load(surface_flux, flux),
    ]
    first += [
        load(send_list.at[0, :, pl.ds(j * cols_dev, cols_dev)], sends.at[:, j]) for j in range(per)
    ]
    third = [load(layer_mass, lm)]
    fourth = [
        load(ocean_state.at[3:5], tracers),
        load(map_slot, slots),
        load(map_weight, weights),
    ]

    for guard in (0, bottom + HALO):
        state[:, guard : guard + GUARD, :] = jnp.zeros((4, GUARD, state.shape[2]), jnp.float32)
        flux_n[guard : guard + GUARD, :] = jnp.zeros((GUARD, state.shape[2]), jnp.float32)

    def halo_copies(cells, pack, halo, send_sem, recv_sem):
        up = lax.rem(comp + n_comp - 1, n_comp)
        down = lax.rem(comp + 1, n_comp)
        right = lax.rem(sub + 1, n_sub)
        left = lax.rem(sub + n_sub - 1, n_sub)
        wide = pl.ds(0, cols_dev)
        plan = [
            (
                cells.at[:, pl.ds(bottom - HALO, HALO), wide],
                cells.at[:, pl.ds(GUARD, HALO), wide],
                (down, sub),
            ),
            (
                cells.at[:, pl.ds(TOP, HALO), wide],
                cells.at[:, pl.ds(bottom, HALO), wide],
                (up, sub),
            ),
        ]
        for side, there in ((0, right), (1, left)):
            plan += [
                (pack.at[side], halo.at[side, pl.ds(HALO, rows_dev)], (comp, there)),
                (
                    pack.at[side, pl.ds(rows_dev - HALO, HALO)],
                    halo.at[side, pl.ds(0, HALO)],
                    (down, there),
                ),
                (
                    pack.at[side, pl.ds(0, HALO)],
                    halo.at[side, pl.ds(HALO + rows_dev, HALO)],
                    (up, there),
                ),
            ]
        return [
            pltpu.make_async_remote_copy(
                src_ref=src,
                dst_ref=dst,
                send_sem=send_sem.at[i],
                recv_sem=recv_sem.at[i],
                device_id={"comp": target[0], "sub": target[1]},
                device_id_type=MESH,
            )
            for i, (src, dst, target) in enumerate(plan)
        ]

    lane_halo = lax.broadcasted_iota(jnp.int32, (rows_dev + 2 * HALO, LANES), 1)

    def pack_edges(cells, count, pack, begin, end):
        lane = lax.broadcasted_iota(jnp.int32, (end - begin, LANES), 1)
        rows = slice(TOP + begin, TOP + end)
        right_edge = cells[0, rows, cols_dev - LANES : cols_dev]
        left_edge = cells[0, rows, 0:LANES]
        for k in range(1, count):
            tile = cells[k, rows, cols_dev - LANES : cols_dev]
            right_edge = jnp.where(
                lane < LANES - k * HALO, pltpu.roll(tile, LANES - k * HALO, 1), right_edge
            )
            tile = cells[k, rows, 0:LANES]
            left_edge = jnp.where(lane >= k * HALO, pltpu.roll(tile, k * HALO, 1), left_edge)
        pack[0, begin:end] = right_edge
        pack[1, begin:end] = left_edge

    def unpack_edges(cells, count, halo):
        from_left = halo[0]
        from_right = halo[1]
        for k in range(count):
            left_k = pltpu.roll(from_left, k * HALO, 1) if k else from_left
            right_k = pltpu.roll(from_right, LANES - k * HALO, 1) if k else from_right
            cells[k, GUARD : bottom + HALO, cols_dev : cols_dev + LANES] = jnp.where(
                lane_halo < LANES // 2, right_k, left_k
            )

    for copy in second:
        copy.wait()
    pack_edges(state, 4, pack_state, 0, rows_dev)
    state_copies = halo_copies(state, pack_state, halo_state, st_send, st_recv)
    for copy in first[:6]:
        copy.wait()
    east = wu[0:1, :].astype(jnp.float32)
    north = wv[0:1, :].astype(jnp.float32)
    dens = ad[0:1, :].astype(jnp.float32)
    buoy = bf[0:1, :].astype(jnp.float32)
    height_sd = oro[0:1, :]
    speed = jnp.sqrt(east * east + north * north)
    inverse = 1.0 / speed
    dir_east = east * inverse
    dir_north = north * inverse
    base = dens * buoy * height_sd * height_sd * speed
    bulk = BULK_SCALE * dens * speed
    surface[0:1, :] = base
    surface[1:2, :] = TEND_SCALE * dir_east
    surface[2:3, :] = TEND_SCALE * dir_north
    sources = [
        base * dir_east + bulk * east,
        base * dir_north + bulk * north,
        flux[0:1, :] + flux[1:2, :] + flux[2:3, :] + flux[3:4, :],
        flux[4:5, :] - flux[5:6, :],
    ]
    field_rows = columns // cols_dev
    for f in range(4):
        for r in range(field_rows):
            fields[r // per, f, r % per : r % per + 1, :] = sources[f][:, r * cols_dev : (r + 1) * cols_dev]

    for copy in first[6:]:
        copy.wait()
    pl.semaphore_wait(barrier, devices - 1)

    def place(d):
        return {"comp": d // n_sub, "sub": lax.rem(d, n_sub)}

    def list_copy(d, at):
        return pltpu.make_async_remote_copy(
            src_ref=sends.at[d],
            dst_ref=tables.at[at],
            send_sem=ix_send.at[d],
            recv_sem=ix_recv.at[at],
            device_id=place(d),
            device_id_type=MESH,
        )

    def send_lists(k, carry):
        list_copy(lax.rem(me + k, devices), me).start()
        return carry


    blocks = fields.shape[0]
    union = stage.shape[1]

    def comp_copy(there, at):
        begin = lax.rem(there * n_sub, blocks)
        return pltpu.make_async_remote_copy(
            src_ref=fields.at[pl.ds(begin, union)],
            dst_ref=stage.at[at],
            send_sem=z_send.at[there],
            recv_sem=z_recv.at[at],
            device_id={"comp": there, "sub": sub},
            device_id_type=MESH,
        )

    def sub_copy(z, there, at):
        return pltpu.make_async_remote_copy(
            src_ref=stage.at[z, lax.rem(there, union)],
            dst_ref=received.at[z * n_sub + at],
            send_sem=a2a_send.at[z * n_sub + there],
            recv_sem=a2a_recv.at[z * n_sub + at],
            device_id={"comp": comp, "sub": there},
            device_id_type=MESH,
        )

    def send_comp(k, carry):
        there = lax.rem(comp + n_comp - k, n_comp)
        comp_copy(there, comp).start()
        return carry

    lax.fori_loop(1, n_comp, send_comp, 0)
    lax.fori_loop(1, devices, send_lists, 0)
    tables[me] = sends[me]
    stage[comp] = fields[pl.ds(lax.rem(comp * n_sub, blocks), union)]

    def hand_on(z):
        for k in range(1, n_sub):
            sub_copy(z, lax.rem(sub + k, n_sub), sub).start()
        received[z * n_sub + sub] = stage[z, lax.rem(sub, union)]

    hand_on(comp)
    for copy in state_copies:
        copy.start()

    total_rows = cor.shape[0]
    row_global = comp * rows_dev - TOP + lax.broadcasted_iota(jnp.int32, cor.shape, 0)
    phase = 2.0 * math.pi * (row_global.astype(jnp.float32) + 0.5) / (rows_dev * n_comp)
    cor[...] = (TIME_STEP * CORIOLIS_MAX) * jnp.cos(phase)

    for copy in third:
        copy.wait()
    width = 2 * LANES
    row8 = lax.broadcasted_iota(jnp.int32, (8, width), 0)

    def drag_chunk(c, carry):
        at = pl.ds(pl.multiple_of(c * width, width), width)
        u = wu[:, at].astype(jnp.float32)
        v = wv[:, at].astype(jnp.float32)
        sq = u * u + v * v
        sat = (
            SAT_SCALE
            * ad[:, at].astype(jnp.float32)
            * (sq * sq * lax.rsqrt(sq))
            / bf[:, at].astype(jnp.float32)
        )
        inv_mass = 1.0 / lm[:, at].astype(jnp.float32)
        above = jnp.broadcast_to(surface[0:1, at], (8, width))
        dir_e = jnp.broadcast_to(surface[1:2, at], (8, width))
        dir_n = jnp.broadcast_to(surface[2:3, at], (8, width))
        out_e = []
        out_n = []
        for lev in range(0, levels, 8):
            low = jnp.minimum(sat[lev : lev + 8], above)
            for shift in (1, 2, 4):
                low = jnp.minimum(low, jnp.where(row8 >= shift, pltpu.roll(low, shift, 0), low))
            below = jnp.where(row8 >= 1, pltpu.roll(low, 1, 0), above)
            change = (low - below) * inv_mass[lev : lev + 8]
            out_e.append(change * dir_e)
            out_n.append(change * dir_n)
            above = jnp.broadcast_to(low[7:8], (8, width))
        drag[0, :, at] = jnp.concatenate(out_e, axis=0).astype(jnp.bfloat16)
        drag[1, :, at] = jnp.concatenate(out_n, axis=0).astype(jnp.bfloat16)
        return carry

    lax.fori_loop(0, columns // width, drag_chunk, 0)
    drag_store = pltpu.make_async_copy(drag, drag_hbm, out_sem.at[0])
    drag_store.start()

    def pass_on(k, carry):
        z = lax.rem(comp + k, n_comp)
        comp_copy(z, z).wait_recv()
        hand_on(z)
        return carry

    lax.fori_loop(1, n_comp, pass_on, 0)

    for copy in fourth:
        copy.wait()

    def join(tile, carry):
        for j in range(dpt):
            s = tile * dpt + j

            @pl.when(s != me)
            def _():
                list_copy(s, s).wait_recv()

        rows = pl.ds(pl.multiple_of(tile * 8, 8), 8)
        table = jnp.concatenate([tables[tile * dpt + j] for j in range(dpt)], axis=0) & (LANES - 1)
        for k in range(slots.shape[0]):
            slots[k, rows, :] = gather_row_tile(table, slots[k, rows, :] & (LANES - 1))
        return carry

    lax.fori_loop(0, tiles, join, 0)

    def spread(tile):
        for j in range(dpt):
            s = tile * dpt + j

            @pl.when(lax.rem(s, n_sub) != sub)
            def _():
                sub_copy(s // n_sub, lax.rem(s, n_sub), lax.rem(s, n_sub)).wait_recv()

        rows = pl.ds(pl.multiple_of(tile * 8, 8), 8)
        rows_in = pl.ds(pl.multiple_of(TOP + tile * 8, 8), 8)
        wide = pl.ds(0, cols_dev)
        idx = [slots[k, rows, :] for k in range(slots.shape[0])]
        wgt = [weights[k, rows, :] for k in range(slots.shape[0])]
        forcing = []
        for f in range(4):
            values = jnp.concatenate([received[tile * dpt + j, f] for j in range(dpt)], axis=0)
            terms = [w * gather_row_tile(values, x) for w, x in zip(wgt, idx)]
            forcing.append(sum(terms[1:], terms[0]))
        scale = (TIME_STEP * WIND_PUSH) / state[3, rows_in, wide]
        push[0, rows_in, wide] = forcing[0] * scale
        push[1, rows_in, wide] = forcing[1] * scale
        tracers[0, rows, :] = tracers[0, rows, :] + HEAT_RATE * forcing[2]
        tracers[1, rows, :] = tracers[1, rows, :] - SALT_RATE * forcing[3]

    edge = HALO // 8
    inner = tiles - 2 * edge

    def spread_edge(i, carry):
        spread(jnp.where(i < edge, i, i + inner))
        return carry

    def spread_inner(i, carry):
        spread(edge + lax.rem(me // dpt + 2 * inner - i, inner))
        return carry

    push_copies = halo_copies(push, pack_push, halo_push, pu_send, pu_recv)
    lax.fori_loop(0, 2 * edge, spread_edge, 0)
    pack_edges(push, 2, pack_push, 0, HALO)
    pack_edges(push, 2, pack_push, rows_dev - HALO, rows_dev)
    for i in (0, 1, 3, 4, 6, 7):
        push_copies[i].start()
    lax.fori_loop(0, inner, spread_inner, 0)
    pack_edges(push, 2, pack_push, HALO, rows_dev - HALO)
    for i in (2, 5):
        push_copies[i].start()
    tracer_store = pltpu.make_async_copy(tracers, ocean_hbm.at[3:5], out_sem.at[1])
    tracer_store.start()
    for copy in state_copies:
        copy.wait_recv()
    unpack_edges(state, 4, halo_state)
    for copy in state_copies:
        copy.wait_send()
    for copy in push_copies:
        copy.wait()
    unpack_edges(push, 2, halo_push)

    span = state.shape[2]
    keep = 1.0 - TIME_STEP * BOTTOM_DRAG
    half = 0.5 * TIME_STEP
    copies = span // LANES

    def diff_east(a):
        return pltpu.roll(a, span - 1, 1) - pltpu.roll(a, 1, 1)

    def step(margin, n, carry):
        chunk = rows_dev // 2 + margin
        for a in range(TOP - margin, bottom + margin, chunk):
            h = state[0, a : a + chunk, :]
            u = state[1, a : a + chunk, :]
            v = state[2, a : a + chunk, :]
            d = state[3, a : a + chunk, :]
            turn = jnp.concatenate([cor[a : a + chunk, :]] * copies, axis=1)
            grad_n = state[0, a + 1 : a + chunk + 1, :] - state[0, a - 1 : a + chunk - 1, :]
            new_u = keep * u + turn * v - half * diff_east(h) + push[0, a : a + chunk, :]
            new_v = keep * v - turn * u - half * grad_n + push[1, a : a + chunk, :]
            state[1, a : a + chunk, :] = new_u
            state[2, a : a + chunk, :] = new_v
            flux_n[a : a + chunk, :] = d * new_v
            height_x[a : a + chunk, :] = h - half * diff_east(d * new_u)
        for a in range(TOP - margin, bottom + margin, chunk):
            div_n = flux_n[a + 1 : a + chunk + 1, :] - flux_n[a - 1 : a + chunk - 1, :]
            state[0, a : a + chunk, :] = height_x[a : a + chunk, :] - half * div_n
        return carry

    lax.fori_loop(0, SUBCYCLES // 2, functools.partial(step, HALO), 0)
    lax.fori_loop(SUBCYCLES // 2, SUBCYCLES, functools.partial(step, HALO // 2), 0)
    ocean_store = pltpu.make_async_copy(
        state.at[0:3, pl.ds(TOP, rows_dev), pl.ds(0, cols_dev)], ocean_hbm.at[0:3], out_sem.at[2]
    )
    ocean_store.start()

    def drain(k, carry):
        list_copy(lax.rem(me + k, devices), me).wait_send()
        return carry

    def drain_comp(k, carry):
        comp_copy(lax.rem(comp + k, n_comp), comp).wait_send()
        return carry

    def drain_sub(z, carry):
        for k in range(1, n_sub):
            sub_copy(z, lax.rem(sub + k, n_sub), sub).wait_send()
        return carry

    lax.fori_loop(1, n_comp, drain_comp, 0)
    lax.fori_loop(0, n_comp, drain_sub, 0)

    lax.fori_loop(1, devices, drain, 0)
    drag_store.wait()
    tracer_store.wait()
    ocean_store.wait()


def shards(n_comp, n_sub, *args):
    wind_u, orography, surface_flux, send_list = args[0], args[5], args[6], args[7]
    depth, ocean_state, map_slot, map_weight = args[8:12]
    devices = n_comp * n_sub
    levels, columns = wind_u.shape
    rows_dev, cols_dev = depth.shape
    entries = map_slot.shape[0]
    cap = send_list.shape[2]
    per = cap // cols_dev
    blocks = columns // (cols_dev * per)
    total_rows = rows_dev + 2 * TOP
    span = cols_dev + LANES
    halo_rows = rows_dev + 2 * HALO
    f32 = jnp.float32
    air = pltpu.VMEM((levels, columns), jnp.bfloat16)
    args = args[:5] + (orography.reshape(1, -1),) + args[6:]
    dma = pltpu.SemaphoreType.DMA
    return pl.pallas_call(
        functools.partial(kernel, n_comp, n_sub),
        out_shape=(
            pltpu.VMEM((2, levels, columns), jnp.bfloat16),
            jax.ShapeDtypeStruct(ocean_state.shape, f32),
        ),
        in_specs=[pl.BlockSpec(memory_space=pltpu.HBM)] * 12,
        out_specs=[pl.BlockSpec(memory_space=pltpu.HBM)] * 2,
        scratch_shapes=[
            air,
            air,
            air,
            air,
            air,
            pltpu.VMEM((1, columns), f32),
            pltpu.VMEM(surface_flux.shape, f32),
            pltpu.VMEM((devices, per, cols_dev), jnp.int32),
            pltpu.VMEM((entries, rows_dev, cols_dev), jnp.int32),
            pltpu.VMEM((entries, rows_dev, cols_dev), f32),
            pltpu.VMEM((2, rows_dev, cols_dev), f32),
            pltpu.VMEM((2, levels, columns), jnp.bfloat16),
            pltpu.VMEM((8, columns), f32),
            pltpu.VMEM((blocks, 4, per, cols_dev), f32),
            pltpu.VMEM((devices, per, cols_dev), jnp.int32),
            pltpu.VMEM((n_comp, min(blocks, n_sub), 4, per, cols_dev), f32),
            pltpu.VMEM((devices, 4, per, cols_dev), f32),
            pltpu.VMEM((4, total_rows, span), f32),
            pltpu.VMEM((2, total_rows, span), f32),
            pltpu.VMEM((total_rows, LANES), f32),
            pltpu.VMEM((total_rows, span), f32),
            pltpu.VMEM((total_rows, span), f32),
            pltpu.VMEM((2, rows_dev, LANES), f32),
            pltpu.VMEM((2, halo_rows, LANES), f32),
            pltpu.VMEM((2, rows_dev, LANES), f32),
            pltpu.VMEM((2, halo_rows, LANES), f32),
            dma((12 + per,)),
            dma((3,)),
            dma((devices,)),
            dma((devices,)),
            dma((n_comp,)),
            dma((n_comp,)),
            dma((devices,)),
            dma((devices,)),
            dma((8,)),
            dma((8,)),
            dma((8,)),
            dma((8,)),
        ],
        compiler_params=pltpu.CompilerParams(
            collective_id=0, has_side_effects=True, vmem_limit_bytes=58 * 1024 * 1024
        ),
    )(*args)


def solution(mesh):
    return jax.shard_map(
        functools.partial(shards, mesh.shape["comp"], mesh.shape["sub"]),
        mesh=mesh,
        in_specs=(
            P(None, ("group", "comp", "sub")),
            P(None, ("group", "comp", "sub")),
            P(None, ("group", "comp", "sub")),
            P(None, ("group", "comp", "sub")),
            P(None, ("group", "comp", "sub")),
            P(("comp", "sub")),
            P(None, ("group", "comp", "sub")),
            P(("comp", "sub"), None, None),
            P("comp", "sub"),
            P(None, ("group", "comp"), "sub"),
            P(None, "comp", "sub"),
            P(None, "comp", "sub"),
        ),
        out_specs=(P(None, None, ("group", "comp", "sub")), P(None, ("group", "comp"), "sub")),
        check_vma=False,
    )
```

```python
import functools
import math

import jax
import jax.numpy as jnp
from jax import lax
from jax.experimental import pallas as pl
from jax.experimental.pallas import tpu as pltpu
from jax.sharding import PartitionSpec as P

SUBCYCLES = 8

SAT_SCALE = 0.1
BULK_SCALE = 0.2
TEND_SCALE = 8.0
WIND_PUSH = 0.1
HEAT_RATE = 0.2
SALT_RATE = 0.3
TIME_STEP = 0.6
BOTTOM_DRAG = 0.05
CORIOLIS_MAX = 0.2

LANES = 128
HALO = 2 * SUBCYCLES
GUARD = 8
TOP = GUARD + HALO
MESH = pl.DeviceIdType.MESH


def lane_gather(values, idx):
    return jnp.take_along_axis(values, idx, axis=1, mode="promise_in_bounds")


def gather_row_tile(values, idx):
    halves = [
        lane_gather(values[:, at : at + LANES], idx[:, at : at + LANES])
        for at in range(0, values.shape[1], LANES)
    ]
    return jnp.concatenate(halves, axis=1)


def kernel(
    n_comp,
    n_sub,
    wind_u,
    wind_v,
    buoyancy_freq,
    air_density,
    layer_mass,
    orography,
    surface_flux,
    send_list,
    depth,
    ocean_state,
    map_slot,
    map_weight,
    drag_hbm,
    ocean_hbm,
    wu,
    wv,
    bf,
    ad,
    lm,
    oro,
    flux,
    sends,
    slots,
    weights,
    tracers,
    drag,
    surface,
    fields,
    tables,
    stage,
    received,
    state,
    push,
    cor,
    flux_n,
    height_x,
    pack_state,
    halo_state,
    pack_push,
    halo_push,
    in_sem,
    out_sem,
    ix_send,
    ix_recv,
    z_send,
    z_recv,
    a2a_send,
    a2a_recv,
    st_send,
    st_recv,
    pu_send,
    pu_recv,
):
    devices = n_comp * n_sub
    comp = lax.axis_index("comp")
    sub = lax.axis_index("sub")
    me = comp * n_sub + sub
    rows_dev, cols_dev = depth.shape
    per = sends.shape[1]
    dpt = 8 // per
    tiles = devices // dpt
    bottom = TOP + rows_dev
    levels, columns = wu.shape

    barrier = pltpu.get_barrier_semaphore()

    def greet(k, carry):
        d = lax.rem(me + k, devices)
        pl.semaphore_signal(
            barrier, inc=1, device_id={"comp": d // n_sub, "sub": lax.rem(d, n_sub)}, device_id_type=MESH
        )
        return carry

    lax.fori_loop(1, devices, greet, 0)

    loads = []

    def load(src, dst):
        copy = pltpu.make_async_copy(src, dst, in_sem.at[len(loads)])
        copy.start()
        loads.append(copy)
        return copy

    second = [
        load(ocean_state.at[0:3], state.at[0:3, pl.ds(TOP, rows_dev), pl.ds(0, cols_dev)]),
        load(depth, state.at[3, pl.ds(TOP, rows_dev), pl.ds(0, cols_dev)]),
    ]
    first = [
        load(wind_u, wu),
        load(wind_v, wv),
        load(buoyancy_freq, bf),
        load(air_density, ad),
        load(orography, oro),
        load(surface_flux, flux),
    ]
    first += [
        load(send_list.at[0, :, pl.ds(j * cols_dev, cols_dev)], sends.at[:, j]) for j in range(per)
    ]
    third = [load(layer_mass, lm)]
    fourth = [
        load(ocean_state.at[3:5], tracers),
        load(map_slot, slots),
        load(map_weight, weights),
    ]

    for guard in (0, bottom + HALO):
        state[:, guard : guard + GUARD, :] = jnp.zeros((4, GUARD, state.shape[2]), jnp.float32)
        flux_n[guard : guard + GUARD, :] = jnp.zeros((GUARD, state.shape[2]), jnp.float32)

    def halo_copies(cells, pack, halo, send_sem, recv_sem):
        up = lax.rem(comp + n_comp - 1, n_comp)
        down = lax.rem(comp + 1, n_comp)
        right = lax.rem(sub + 1, n_sub)
        left = lax.rem(sub + n_sub - 1, n_sub)
        wide = pl.ds(0, cols_dev)
        plan = [
            (
                cells.at[:, pl.ds(bottom - HALO, HALO), wide],
                cells.at[:, pl.ds(GUARD, HALO), wide],
                (down, sub),
            ),
            (
                cells.at[:, pl.ds(TOP, HALO), wide],
                cells.at[:, pl.ds(bottom, HALO), wide],
                (up, sub),
            ),
        ]
        for side, there in ((0, right), (1, left)):
            plan += [
                (pack.at[side], halo.at[side, pl.ds(HALO, rows_dev)], (comp, there)),
                (
                    pack.at[side, pl.ds(rows_dev - HALO, HALO)],
                    halo.at[side, pl.ds(0, HALO)],
                    (down, there),
                ),
                (
                    pack.at[side, pl.ds(0, HALO)],
                    halo.at[side, pl.ds(HALO + rows_dev, HALO)],
                    (up, there),
                ),
            ]
        return [
            pltpu.make_async_remote_copy(
                src_ref=src,
                dst_ref=dst,
                send_sem=send_sem.at[i],
                recv_sem=recv_sem.at[i],
                device_id={"comp": target[0], "sub": target[1]},
                device_id_type=MESH,
            )
            for i, (src, dst, target) in enumerate(plan)
        ]

    lane_halo = lax.broadcasted_iota(jnp.int32, (rows_dev + 2 * HALO, LANES), 1)

    def pack_edges(cells, count, pack, begin, end):
        lane = lax.broadcasted_iota(jnp.int32, (end - begin, LANES), 1)
        rows = slice(TOP + begin, TOP + end)
        right_edge = cells[0, rows, cols_dev - LANES : cols_dev]
        left_edge = cells[0, rows, 0:LANES]
        for k in range(1, count):
            tile = cells[k, rows, cols_dev - LANES : cols_dev]
            right_edge = jnp.where(
                lane < LANES - k * HALO, pltpu.roll(tile, LANES - k * HALO, 1), right_edge
            )
            tile = cells[k, rows, 0:LANES]
            left_edge = jnp.where(lane >= k * HALO, pltpu.roll(tile, k * HALO, 1), left_edge)
        pack[0, begin:end] = right_edge
        pack[1, begin:end] = left_edge

    def unpack_edges(cells, count, halo):
        from_left = halo[0]
        from_right = halo[1]
        for k in range(count):
            left_k = pltpu.roll(from_left, k * HALO, 1) if k else from_left
            right_k = pltpu.roll(from_right, LANES - k * HALO, 1) if k else from_right
            cells[k, GUARD : bottom + HALO, cols_dev : cols_dev + LANES] = jnp.where(
                lane_halo < LANES // 2, right_k, left_k
            )

    for copy in second:
        copy.wait()
    pack_edges(state, 4, pack_state, 0, rows_dev)
    state_copies = halo_copies(state, pack_state, halo_state, st_send, st_recv)
    for copy in first[:6]:
        copy.wait()
    east = wu[0:1, :].astype(jnp.float32)
    north = wv[0:1, :].astype(jnp.float32)
    dens = ad[0:1, :].astype(jnp.float32)
    buoy = bf[0:1, :].astype(jnp.float32)
    height_sd = oro[0:1, :]
    speed = jnp.sqrt(east * east + north * north)
    inverse = 1.0 / speed
    dir_east = east * inverse
    dir_north = north * inverse
    base = dens * buoy * height_sd * height_sd * speed
    bulk = BULK_SCALE * dens * speed
    surface[0:1, :] = base
    surface[1:2, :] = TEND_SCALE * dir_east
    surface[2:3, :] = TEND_SCALE * dir_north
    sources = [
        base * dir_east + bulk * east,
        base * dir_north + bulk * north,
        flux[0:1, :] + flux[1:2, :] + flux[2:3, :] + flux[3:4, :],
        flux[4:5, :] - flux[5:6, :],
    ]
    field_rows = columns // cols_dev
    for f in range(4):
        for r in range(field_rows):
            fields[r // per, f, r % per : r % per + 1, :] = sources[f][:, r * cols_dev : (r + 1) * cols_dev]

    for copy in first[6:]:
        copy.wait()
    pl.semaphore_wait(barrier, devices - 1)

    def place(d):
        return {"comp": d // n_sub, "sub": lax.rem(d, n_sub)}

    def list_copy(d, at):
        return pltpu.make_async_remote_copy(
            src_ref=sends.at[d],
            dst_ref=tables.at[at],
            send_sem=ix_send.at[d],
            recv_sem=ix_recv.at[at],
            device_id=place(d),
            device_id_type=MESH,
        )

    def send_lists(k, carry):
        list_copy(lax.rem(me + k, devices), me).start()
        return carry


    blocks = fields.shape[0]
    union = stage.shape[1]

    def comp_copy(there, at):
        begin = lax.rem(there * n_sub, blocks)
        return pltpu.make_async_remote_copy(
            src_ref=fields.at[pl.ds(begin, union)],
            dst_ref=stage.at[at],
            send_sem=z_send.at[there],
            recv_sem=z_recv.at[at],
            device_id={"comp": there, "sub": sub},
            device_id_type=MESH,
        )

    def sub_copy(z, there, at):
        return pltpu.make_async_remote_copy(
            src_ref=stage.at[z, lax.rem(there, union)],
            dst_ref=received.at[z * n_sub + at],
            send_sem=a2a_send.at[z * n_sub + there],
            recv_sem=a2a_recv.at[z * n_sub + at],
            device_id={"comp": comp, "sub": there},
            device_id_type=MESH,
        )

    def send_comp(k, carry):
        there = lax.rem(comp + n_comp - k, n_comp)
        comp_copy(there, comp).start()
        return carry

    lax.fori_loop(1, n_comp, send_comp, 0)
    lax.fori_loop(1, devices, send_lists, 0)
    tables[me] = sends[me]
    stage[comp] = fields[pl.ds(lax.rem(comp * n_sub, blocks), union)]

    def hand_on(z):
        for k in range(1, n_sub):
            sub_copy(z, lax.rem(sub + k, n_sub), sub).start()
        received[z * n_sub + sub] = stage[z, lax.rem(sub, union)]

    hand_on(comp)

    total_rows = cor.shape[0]
    row_global = comp * rows_dev - TOP + lax.broadcasted_iota(jnp.int32, cor.shape, 0)
    phase = 2.0 * math.pi * (row_global.astype(jnp.float32) + 0.5) / (rows_dev * n_comp)
    cor[...] = (TIME_STEP * CORIOLIS_MAX) * jnp.cos(phase)

    for copy in third:
        copy.wait()
    width = 2 * LANES
    row8 = lax.broadcasted_iota(jnp.int32, (8, width), 0)

    def drag_chunk(c, carry):
        at = pl.ds(pl.multiple_of(c * width, width), width)
        u = wu[:, at].astype(jnp.float32)
        v = wv[:, at].astype(jnp.float32)
        sq = u * u + v * v
        sat = (
            SAT_SCALE
            * ad[:, at].astype(jnp.float32)
            * (sq * sq * lax.rsqrt(sq))
            / bf[:, at].astype(jnp.float32)
        )
        inv_mass = 1.0 / lm[:, at].astype(jnp.float32)
        above = jnp.broadcast_to(surface[0:1, at], (8, width))
        dir_e = jnp.broadcast_to(surface[1:2, at], (8, width))
        dir_n = jnp.broadcast_to(surface[2:3, at], (8, width))
        out_e = []
        out_n = []
        for lev in range(0, levels, 8):
            low = jnp.minimum(sat[lev : lev + 8], above)
            for shift in (1, 2, 4):
                low = jnp.minimum(low, jnp.where(row8 >= shift, pltpu.roll(low, shift, 0), low))
            below = jnp.where(row8 >= 1, pltpu.roll(low, 1, 0), above)
            change = (low - below) * inv_mass[lev : lev + 8]
            out_e.append(change * dir_e)
            out_n.append(change * dir_n)
            above = jnp.broadcast_to(low[7:8], (8, width))
        drag[0, :, at] = jnp.concatenate(out_e, axis=0).astype(jnp.bfloat16)
        drag[1, :, at] = jnp.concatenate(out_n, axis=0).astype(jnp.bfloat16)
        return carry

    lax.fori_loop(0, columns // width // 2, drag_chunk, 0)
    def pass_on(k, carry):
        z = lax.rem(comp + k, n_comp)
        comp_copy(z, z).wait_recv()
        hand_on(z)
        return carry

    lax.fori_loop(1, n_comp, pass_on, 0)
    for copy in state_copies:
        copy.start()
    lax.fori_loop(columns // width // 2, columns // width, drag_chunk, 0)
    drag_store = pltpu.make_async_copy(drag, drag_hbm, out_sem.at[0])
    drag_store.start()

    for copy in fourth:
        copy.wait()

    def join(tile, carry):
        for j in range(dpt):
            s = tile * dpt + j

            @pl.when(s != me)
            def _():
                list_copy(s, s).wait_recv()

        rows = pl.ds(pl.multiple_of(tile * 8, 8), 8)
        table = jnp.concatenate([tables[tile * dpt + j] for j in range(dpt)], axis=0) & (LANES - 1)
        for k in range(slots.shape[0]):
            slots[k, rows, :] = gather_row_tile(table, slots[k, rows, :] & (LANES - 1))
        return carry

    lax.fori_loop(0, tiles, join, 0)

    def spread(tile):
        for j in range(dpt):
            s = tile * dpt + j

            @pl.when(lax.rem(s, n_sub) != sub)
            def _():
                sub_copy(s // n_sub, lax.rem(s, n_sub), lax.rem(s, n_sub)).wait_recv()

        rows = pl.ds(pl.multiple_of(tile * 8, 8), 8)
        rows_in = pl.ds(pl.multiple_of(TOP + tile * 8, 8), 8)
        wide = pl.ds(0, cols_dev)
        idx = [slots[k, rows, :] for k in range(slots.shape[0])]
        wgt = [weights[k, rows, :] for k in range(slots.shape[0])]
        forcing = []
        for f in range(4):
            values = jnp.concatenate([received[tile * dpt + j, f] for j in range(dpt)], axis=0)
            terms = [w * gather_row_tile(values, x) for w, x in zip(wgt, idx)]
            forcing.append(sum(terms[1:], terms[0]))
        scale = (TIME_STEP * WIND_PUSH) / state[3, rows_in, wide]
        push[0, rows_in, wide] = forcing[0] * scale
        push[1, rows_in, wide] = forcing[1] * scale
        tracers[0, rows, :] = tracers[0, rows, :] + HEAT_RATE * forcing[2]
        tracers[1, rows, :] = tracers[1, rows, :] - SALT_RATE * forcing[3]

    edge = HALO // 8
    inner = tiles - 2 * edge

    def spread_edge(i, carry):
        spread(jnp.where(i < edge, i, i + inner))
        return carry

    def spread_inner(i, carry):
        spread(edge + lax.rem(me // dpt + 2 * inner - i, inner))
        return carry

    push_copies = halo_copies(push, pack_push, halo_push, pu_send, pu_recv)
    lax.fori_loop(0, 2 * edge, spread_edge, 0)
    pack_edges(push, 2, pack_push, 0, HALO)
    pack_edges(push, 2, pack_push, rows_dev - HALO, rows_dev)
    for i in (0, 1, 3, 4, 6, 7):
        push_copies[i].start()
    lax.fori_loop(0, inner, spread_inner, 0)
    pack_edges(push, 2, pack_push, HALO, rows_dev - HALO)
    for i in (2, 5):
        push_copies[i].start()
    tracer_store = pltpu.make_async_copy(tracers, ocean_hbm.at[3:5], out_sem.at[1])
    tracer_store.start()
    for copy in state_copies:
        copy.wait_recv()
    unpack_edges(state, 4, halo_state)
    for copy in state_copies:
        copy.wait_send()
    for copy in push_copies:
        copy.wait()
    unpack_edges(push, 2, halo_push)

    span = state.shape[2]
    keep = 1.0 - TIME_STEP * BOTTOM_DRAG
    half = 0.5 * TIME_STEP
    copies = span // LANES

    def diff_east(a):
        return pltpu.roll(a, span - 1, 1) - pltpu.roll(a, 1, 1)

    def step(margin, n, carry):
        chunk = rows_dev // 2 + margin
        for a in range(TOP - margin, bottom + margin, chunk):
            h = state[0, a : a + chunk, :]
            u = state[1, a : a + chunk, :]
            v = state[2, a : a + chunk, :]
            d = state[3, a : a + chunk, :]
            turn = jnp.concatenate([cor[a : a + chunk, :]] * copies, axis=1)
            grad_n = state[0, a + 1 : a + chunk + 1, :] - state[0, a - 1 : a + chunk - 1, :]
            new_u = keep * u + turn * v - half * diff_east(h) + push[0, a : a + chunk, :]
            new_v = keep * v - turn * u - half * grad_n + push[1, a : a + chunk, :]
            state[1, a : a + chunk, :] = new_u
            state[2, a : a + chunk, :] = new_v
            flux_n[a : a + chunk, :] = d * new_v
            height_x[a : a + chunk, :] = h - half * diff_east(d * new_u)
        for a in range(TOP - margin, bottom + margin, chunk):
            div_n = flux_n[a + 1 : a + chunk + 1, :] - flux_n[a - 1 : a + chunk - 1, :]
            state[0, a : a + chunk, :] = height_x[a : a + chunk, :] - half * div_n
        return carry

    lax.fori_loop(0, SUBCYCLES // 2, functools.partial(step, HALO), 0)
    lax.fori_loop(SUBCYCLES // 2, SUBCYCLES, functools.partial(step, HALO // 2), 0)
    ocean_store = pltpu.make_async_copy(
        state.at[0:3, pl.ds(TOP, rows_dev), pl.ds(0, cols_dev)], ocean_hbm.at[0:3], out_sem.at[2]
    )
    ocean_store.start()

    def drain(k, carry):
        list_copy(lax.rem(me + k, devices), me).wait_send()
        return carry

    def drain_comp(k, carry):
        comp_copy(lax.rem(comp + k, n_comp), comp).wait_send()
        return carry

    def drain_sub(z, carry):
        for k in range(1, n_sub):
            sub_copy(z, lax.rem(sub + k, n_sub), sub).wait_send()
        return carry

    lax.fori_loop(1, n_comp, drain_comp, 0)
    lax.fori_loop(0, n_comp, drain_sub, 0)

    lax.fori_loop(1, devices, drain, 0)
    drag_store.wait()
    tracer_store.wait()
    ocean_store.wait()


def shards(n_comp, n_sub, *args):
    wind_u, orography, surface_flux, send_list = args[0], args[5], args[6], args[7]
    depth, ocean_state, map_slot, map_weight = args[8:12]
    devices = n_comp * n_sub
    levels, columns = wind_u.shape
    rows_dev, cols_dev = depth.shape
    entries = map_slot.shape[0]
    cap = send_list.shape[2]
    per = cap // cols_dev
    blocks = columns // (cols_dev * per)
    total_rows = rows_dev + 2 * TOP
    span = cols_dev + LANES
    halo_rows = rows_dev + 2 * HALO
    f32 = jnp.float32
    air = pltpu.VMEM((levels, columns), jnp.bfloat16)
    args = args[:5] + (orography.reshape(1, -1),) + args[6:]
    dma = pltpu.SemaphoreType.DMA
    return pl.pallas_call(
        functools.partial(kernel, n_comp, n_sub),
        out_shape=(
            pltpu.VMEM((2, levels, columns), jnp.bfloat16),
            jax.ShapeDtypeStruct(ocean_state.shape, f32),
        ),
        in_specs=[pl.BlockSpec(memory_space=pltpu.HBM)] * 12,
        out_specs=[pl.BlockSpec(memory_space=pltpu.HBM)] * 2,
        scratch_shapes=[
            air,
            air,
            air,
            air,
            air,
            pltpu.VMEM((1, columns), f32),
            pltpu.VMEM(surface_flux.shape, f32),
            pltpu.VMEM((devices, per, cols_dev), jnp.int32),
            pltpu.VMEM((entries, rows_dev, cols_dev), jnp.int32),
            pltpu.VMEM((entries, rows_dev, cols_dev), f32),
            pltpu.VMEM((2, rows_dev, cols_dev), f32),
            pltpu.VMEM((2, levels, columns), jnp.bfloat16),
            pltpu.VMEM((8, columns), f32),
            pltpu.VMEM((blocks, 4, per, cols_dev), f32),
            pltpu.VMEM((devices, per, cols_dev), jnp.int32),
            pltpu.VMEM((n_comp, min(blocks, n_sub), 4, per, cols_dev), f32),
            pltpu.VMEM((devices, 4, per, cols_dev), f32),
            pltpu.VMEM((4, total_rows, span), f32),
            pltpu.VMEM((2, total_rows, span), f32),
            pltpu.VMEM((total_rows, LANES), f32),
            pltpu.VMEM((total_rows, span), f32),
            pltpu.VMEM((total_rows, span), f32),
            pltpu.VMEM((2, rows_dev, LANES), f32),
            pltpu.VMEM((2, halo_rows, LANES), f32),
            pltpu.VMEM((2, rows_dev, LANES), f32),
            pltpu.VMEM((2, halo_rows, LANES), f32),
            dma((12 + per,)),
            dma((3,)),
            dma((devices,)),
            dma((devices,)),
            dma((n_comp,)),
            dma((n_comp,)),
            dma((devices,)),
            dma((devices,)),
            dma((8,)),
            dma((8,)),
            dma((8,)),
            dma((8,)),
        ],
        compiler_params=pltpu.CompilerParams(
            collective_id=0, has_side_effects=True, vmem_limit_bytes=58 * 1024 * 1024
        ),
    )(*args)


def solution(mesh):
    return jax.shard_map(
        functools.partial(shards, mesh.shape["comp"], mesh.shape["sub"]),
        mesh=mesh,
        in_specs=(
            P(None, ("group", "comp", "sub")),
            P(None, ("group", "comp", "sub")),
            P(None, ("group", "comp", "sub")),
            P(None, ("group", "comp", "sub")),
            P(None, ("group", "comp", "sub")),
            P(("comp", "sub")),
            P(None, ("group", "comp", "sub")),
            P(("comp", "sub"), None, None),
            P("comp", "sub"),
            P(None, ("group", "comp"), "sub"),
            P(None, "comp", "sub"),
            P(None, "comp", "sub"),
        ),
        out_specs=(P(None, None, ("group", "comp", "sub")), P(None, ("group", "comp"), "sub")),
        check_vma=False,
    )
```
